32 devices in a mesh: dp: 2 (over core), row: 4 (over z), col: 4 (over y, x).
Axes of the slice: x: 2, y: 2, z: 4, core: 2. Of those that a mesh axis runs over, the one named last changes fastest.
Arguments:
- tokens: bfloat16 [2048, 4096], P(('dp', 'col'), 'row'), may hold values from -6 to 6
- w_in: bfloat16 [4096, 16384], P('row', 'col'), may hold values from -0.09375 to 0.09375
- w_out: bfloat16 [16384, 4096], P('col', 'row'), may hold values from -0.046875 to 0.046875
- out_grad: bfloat16 [2048, 4096], P(('dp', 'col'), 'row'), may hold values from -6 to 6
Outputs:
- output: bfloat16 [2048, 4096], P(('dp', 'col'), 'row')
- grad_x: bfloat16 [2048, 4096], P(('dp', 'col'), 'row')
- grad_w_in: bfloat16 [4096, 4, 4096], P('row', 'col', 'dp')
- grad_w_out: bfloat16 [4, 4096, 4096], P('col', 'dp', 'row')
The draws below stay inside these ranges and needn't reach their ends.
All inputs are finite; a program needn't handle non-finite values.
Results may differ from the reference program's by a relative error of at most 0.005.
Values may be sent and summed in bfloat16 or wider, within the bound.
No kernel may reach another device: no remote copies, remote signals or barrier semaphores. Data moves between devices by JAX's collectives and lax.ppermute only.
A program may use at most 128 MiB of HBM per device.

```python
import math
import jax
import jax.numpy as jnp

D = 4096
FF = 16384
TOKENS = 2048
N_COL = 4


def block_levels(rng, extent, split, least, high):
    level, own = 1.0, jax.random.fold_in(rng, 6)
    for axis_at, parts in split:
        heights = jnp.exp(jax.random.uniform(jax.random.fold_in(own, axis_at), (parts,), jnp.float32, least / len(split), high / len(split)))
        level = level * jnp.repeat(heights, extent[axis_at] // parts).reshape([-1 if axis == axis_at else 1 for axis in range(len(extent))])
    return level


def normal_values(rng, shape, scale, most, split=(), kind=jnp.bfloat16):
    values = jax.random.normal(rng, shape, jnp.float32) * scale
    if len(split) > 0:
        values = block_levels(rng, shape, split, -0.22, 0.18) * values
    return jnp.clip(values, min=-most, max=most).astype(kind)


def setup_inputs(seed: int = 0) -> dict:
    key_of = jax.random.split(jax.random.key(seed), 5)
    return {
        "tokens": normal_values(key_of[0], (TOKENS, D), 1.0, 6.0, ((0, 8), (1, 4))),
        "w_in": normal_values(key_of[1], (D, FF), D ** -0.5, 0.09375, ((0, 4), (1, 4))),
        "w_out": normal_values(key_of[2], (FF, D), FF ** -0.5, 0.046875, ((0, 4), (1, 4))),
        "out_grad": normal_values(key_of[3], (TOKENS, D), 1.0, 6.0, ((0, 8), (1, 4))),
    }


def gelu_parts(pre):
    cdf = 0.5 * (1.0 + jax.scipy.special.erf(pre / math.sqrt(2.0)))
    pdf = jnp.exp(-0.5 * pre * pre) / math.sqrt(2.0 * math.pi)
    return (pre * cdf, cdf + pre * pdf)

def reference(tokens, w_in, w_out, out_grad):
    pre = jnp.dot(tokens, w_in, preferred_element_type=jnp.float32)
    act_value, slope = gelu_parts(pre)
    act = act_value.astype(jnp.bfloat16)
    output = jnp.dot(act, w_out, preferred_element_type=jnp.float32).astype(jnp.bfloat16)
    grad_act = jnp.dot(out_grad, w_out.T, preferred_element_type=jnp.float32)
    grad_pre = (grad_act * slope).astype(jnp.bfloat16)
    grad_x = jnp.dot(grad_pre, w_in.T, preferred_element_type=jnp.float32).astype(jnp.bfloat16)
    gw_in = jnp.dot(tokens.T, grad_pre, preferred_element_type=jnp.float32)
    gw_out = jnp.dot(act.T, out_grad, preferred_element_type=jnp.float32)
    grad_w_in = gw_in.astype(jnp.bfloat16).reshape(D, N_COL, FF // N_COL)
    grad_w_out = gw_out.astype(jnp.bfloat16).reshape(N_COL, FF // N_COL, D)
    return (output, grad_x, grad_w_in, grad_w_out)
```

```python
import functools
import math

import jax
import jax.numpy as jnp
from jax import lax
from jax.experimental import pallas as pl
from jax.experimental.pallas import tpu as pltpu
from jax.sharding import PartitionSpec as P

ROWS = 128
VMEM_MIB = 64
PARTIAL = jnp.bfloat16
ANY = pl.BlockSpec(memory_space=pltpu.HBM)
SMALL = pl.CostEstimate(flops=1024, bytes_accessed=1024, transcendentals=0)


def params(mib):
    return pltpu.CompilerParams(vmem_limit_bytes=mib << 20)


def hbm_out(shape, dtype=jnp.bfloat16):
    return jax.ShapeDtypeStruct(shape, dtype)


def row_chunks(rows):
    parts = 4 if rows % 64 == 0 else 1
    return [(i * (rows // parts), rows // parts) for i in range(parts)]


def across(left, right):
    return lax.dot_general(left, right, (((1,), (1,)), ((), ())), preferred_element_type=jnp.float32)


def project(streams, blocks, weights, replica, hidden, after):
    width = blocks[0][0][0].shape[1]
    tile = min(512, hidden)
    steps = hidden // tile
    operands, specs, out_specs, out_shape = [], [], [], []
    for s in streams:
        if s == 0:
            operands.append(weights[0])
            specs.append(pl.BlockSpec((width, tile), lambda i, d: (0, d[0] * steps + i)))
        else:
            operands.append(weights[1])
            specs.append(pl.BlockSpec((tile, width), lambda i, d: (d[0] * steps + i, 0)))
        for both, first, rows in blocks:
            at = first // rows
            if isinstance(both, tuple):
                operands.append(both[s])
                specs.append(pl.BlockSpec((rows, width), lambda i, d, at=at: (at, 0)))
            else:
                operands.append(both)
                specs.append(pl.BlockSpec((None, rows, width), lambda i, d, s=s, at=at: (s, at, 0)))
            out_specs.append(pl.BlockSpec((rows, tile), lambda i, d: (0, i)))
            out_shape.append(hbm_out((rows, hidden), PARTIAL))

    def body(replica_ref, *refs):
        outs = iter(refs[len(operands) + len(after) :])
        given = iter(refs)
        for s in streams:
            weight = next(given)[...]
            for _ in blocks:
                x = next(given)[...]
                out = next(outs)
                if s == 0:
                    value = jnp.dot(x, weight, preferred_element_type=jnp.float32)
                else:
                    value = across(x, weight)
                out[...] = value.astype(out.dtype)

    done = pl.pallas_call(
        body,
        grid_spec=pltpu.PrefetchScalarGridSpec(
            num_scalar_prefetch=1,
            grid=(steps,),
            in_specs=specs + [ANY] * len(after),
            out_specs=out_specs,
        ),
        out_shape=out_shape,
        compiler_params=params(VMEM_MIB),
        cost_estimate=SMALL,
        name="project",
    )(replica, *operands, *after)
    return [done[i : i + len(blocks)] for i in range(0, len(done), len(blocks))]


def hold(array, after):
    return pl.pallas_call(
        lambda *refs: None,
        in_specs=[ANY] * (1 + len(after)),
        out_specs=ANY,
        out_shape=hbm_out(array.shape, array.dtype),
        input_output_aliases={0: 0},
        compiler_params=params(VMEM_MIB),
        cost_estimate=SMALL,
        name="hold",
    )(array, *after)


def pack(pair, after):
    def body(*refs):
        out, held, in_sem, out_sem = refs[-4:]
        into = [pltpu.make_async_copy(refs[i], held.at[i], in_sem.at[i]) for i in range(2)]
        out_of = [pltpu.make_async_copy(held.at[i], out.at[i], out_sem.at[i]) for i in range(2)]
        for copy in into:
            copy.start()
        for i in range(2):
            into[i].wait()
            out_of[i].start()
        for copy in out_of:
            copy.wait()

    return pl.pallas_call(
        body,
        in_specs=[ANY] * (2 + len(after)),
        out_specs=ANY,
        out_shape=hbm_out((2, *pair[0].shape), pair[0].dtype),
        scratch_shapes=[
            pltpu.VMEM((2, *pair[0].shape), pair[0].dtype),
            pltpu.SemaphoreType.DMA((2,)),
            pltpu.SemaphoreType.DMA((2,)),
        ],
        compiler_params=params(VMEM_MIB),
        cost_estimate=SMALL,
        name="pack",
    )(*pair, *after)


def own_place(ring, line):
    row = lax.axis_index("row")
    return jnp.where(lax.axis_index("dp") == ring, row, line - 1 - row)


def apart(after, arrays):
    return [a for a in after if all(a is not b for b in arrays)]


def distinct(arrays):
    found = []
    for array in arrays:
        if all(array is not seen for seen in found):
            found.append(array)
    return found, [next(i for i, seen in enumerate(found) if seen is a) for a in arrays]


def chain_step(ring, got, partials, after):
    _, rows, hidden = got.shape
    late = len(partials)
    chunks = row_chunks(rows)
    arrays, which = distinct([array for part in partials for array in part[:2]])

    def body(*refs):
        got_h, terms = refs[0], refs[1 : 1 + len(arrays)]
        out_h = refs[1 + len(arrays) + len(after)]
        got_v, own_v, out_v, got_sem, own_sem, out_sem = refs[-6:]
        place = own_place(ring, late)
        copies = []
        for s in range(2):
            for c, (first, count) in enumerate(chunks):
                part = pl.ds(first, count)

                def own_copy(j, s=s, c=c, first=first, count=count, part=part):
                    return pltpu.make_async_copy(
                        terms[which[2 * j + s]].at[pl.ds(partials[j][2] + first, count)],
                        own_v.at[s, part],
                        own_sem.at[s, c],
                    )

                got_copy = pltpu.make_async_copy(
                    got_h.at[s, part], got_v.at[s, part], got_sem.at[s, c]
                )
                out_copy = pltpu.make_async_copy(
                    out_v.at[s, part], out_h.at[s, part], out_sem.at[s, c]
                )
                copies.append((s, part, got_copy, own_copy(0), out_copy))
                got_copy.start()
                for j in range(late):

                    @pl.when(place == j)
                    def _(j=j, own_copy=own_copy):
                        own_copy(j).start()

        for s, part, got_copy, own_copy, out_copy in copies:
            got_copy.wait()
            own_copy.wait()

            @pl.when(place == 0)
            def _(s=s, part=part):
                out_v[s, part] = own_v[s, part].astype(out_v.dtype)

            @pl.when(place != 0)
            def _(s=s, part=part):
                out_v[s, part] = (
                    got_v[s, part].astype(jnp.float32) + own_v[s, part].astype(jnp.float32)
                ).astype(out_v.dtype)

            out_copy.start()
        for copy in copies:
            copy[-1].wait()

    return pl.pallas_call(
        body,
        in_specs=[ANY] * (1 + len(arrays) + len(after)),
        out_specs=ANY,
        out_shape=hbm_out((2, rows, hidden)),
        scratch_shapes=[
            pltpu.VMEM((2, rows, hidden), jnp.bfloat16),
            pltpu.VMEM((2, rows, hidden), PARTIAL),
            pltpu.VMEM((2, rows, hidden), jnp.bfloat16),
        ]
        + [pltpu.SemaphoreType.DMA((2, len(chunks)))] * 3,
        compiler_params=params(VMEM_MIB),
        cost_estimate=SMALL,
        name="chain_step",
    )(got, *arrays, *after)


def activate(partial, got, kept, kept_rows, kept_row, after):
    _, rows, hidden = got[0][0].shape
    line = len(got[0]) + 1
    after = apart(after, kept)
    given, which = distinct([*partial[:2], *got[0], *got[1]])
    step_rows, step_cols = 16, min(512, hidden)
    halves = 2 if rows % 32 == 0 else 1
    part_rows = rows // halves
    across_cols = hidden // step_cols
    tiles = (part_rows // step_rows) * across_cols

    def body(*refs):
        terms = refs[: len(given)]
        outs = refs[len(given) + len(kept) + len(after) :][:2]
        own_v, got_v, out_v, own_sem, got_sem, out_sem = refs[-6:]

        def own_copy(s, h):
            part = pl.ds(h * part_rows, part_rows)
            return pltpu.make_async_copy(
                terms[which[s]].at[pl.ds(partial[2] + h * part_rows, part_rows)],
                own_v.at[s, part],
                own_sem.at[s, h],
            )

        def got_copy(ring, j, s, h):
            part = pl.ds(h * part_rows, part_rows)
            return pltpu.make_async_copy(
                terms[which[2 + ring * (line - 1) + j]].at[s, part],
                got_v.at[ring, s, part],
                got_sem.at[ring, s, h],
            )

        for h in range(halves):
            for s in range(2):
                own_copy(s, h).start()
                for ring in range(2):
                    place = own_place(ring, line)

                    @pl.when(place == 0)
                    def _(ring=ring, s=s, h=h):
                        part = pl.ds(h * part_rows, part_rows)
                        got_v[ring, s, part] = jnp.zeros((part_rows, hidden), got_v.dtype)

                    for j in range(1, line):

                        @pl.when(place == j)
                        def _(ring=ring, j=j, s=s, h=h):
                            got_copy(ring, j - 1, s, h).start()

        out_copies = []
        for h in range(halves):
            for s in range(2):
                own_copy(s, h).wait()
                for ring in range(2):

                    @pl.when(own_place(ring, line) != 0)
                    def _(ring=ring, s=s, h=h):
                        got_copy(ring, 0, s, h).wait()

            def tile(i, _, h=h):
                at = pl.multiple_of((i // across_cols) * step_rows, step_rows)
                r = pl.ds(h * part_rows + at, step_rows)
                c = pl.ds(pl.multiple_of((i % across_cols) * step_cols, step_cols), step_cols)
                pre, grad = (
                    own_v[s, r, c].astype(jnp.float32)
                    + got_v[0, s, r, c].astype(jnp.float32)
                    + got_v[1, s, r, c].astype(jnp.float32)
                    for s in range(2)
                )
                cdf = 0.5 * (1.0 + lax.erf(pre * (1.0 / math.sqrt(2.0))))
                pdf = jnp.exp(-0.5 * pre * pre) * (1.0 / math.sqrt(2.0 * math.pi))
                out_v[0, r, c] = (pre * cdf).astype(jnp.bfloat16)
                out_v[1, r, c] = (grad * (cdf + pre * pdf)).astype(jnp.bfloat16)
                return 0

            lax.fori_loop(0, tiles, tile, 0)
            for i in range(2):
                copy = pltpu.make_async_copy(
                    out_v.at[i, pl.ds(h * part_rows, part_rows)],
                    outs[i].at[pl.ds(kept_row + h * part_rows, part_rows)],
                    out_sem.at[i, h],
                )
                copy.start()
                out_copies.append(copy)
        for copy in out_copies:
            copy.wait()

    return pl.pallas_call(
        body,
        in_specs=[ANY] * (len(given) + len(kept) + len(after)),
        out_specs=[ANY] * 2,
        out_shape=[hbm_out((kept_rows, hidden))] * 2,
        input_output_aliases={len(given) + i: i for i in range(len(kept))},
        scratch_shapes=[
            pltpu.VMEM((2, rows, hidden), PARTIAL),
            pltpu.VMEM((2, 2, rows, hidden), jnp.bfloat16),
            pltpu.VMEM((2, rows, hidden), jnp.bfloat16),
            pltpu.SemaphoreType.DMA((2, halves)),
            pltpu.SemaphoreType.DMA((2, 2, halves)),
            pltpu.SemaphoreType.DMA((2, halves)),
        ],
        compiler_params=params(VMEM_MIB),
        cost_estimate=SMALL,
        name="activate",
    )(*given, *kept, *after)


def share_of(stream, hid, first, rows, weight, after):
    hidden = hid.shape[1]
    width = weight.shape[1 - stream]
    parts = 4 if width % 512 == 0 else 1
    cols = width // parts

    def body(*refs):
        hid_h, weight_h = refs[:2]
        out_h = refs[2 + len(after)]
        hid_v, weight_v, out_v, hid_sem, weight_sem, out_sem = refs[-6:]
        mine = pl.ds(pl.multiple_of(lax.axis_index("dp") * hidden, hidden), hidden)
        hid_copy = pltpu.make_async_copy(hid_h.at[pl.ds(first, rows)], hid_v, hid_sem)
        hid_copy.start()
        weight_copies, out_copies = [], []
        for i in range(parts):
            part = pl.ds(i * cols, cols)
            source = weight_h.at[mine, part] if stream == 0 else weight_h.at[part, mine]
            weight_copies.append(
                pltpu.make_async_copy(source, weight_v.at[i], weight_sem.at[i])
            )
            weight_copies[-1].start()
            out_copies.append(
                pltpu.make_async_copy(out_v.at[:, part], out_h.at[:, part], out_sem.at[i])
            )
        hid_copy.wait()
        for i in range(parts):
            weight_copies[i].wait()
            part = slice(i * cols, (i + 1) * cols)
            if stream == 0:
                out_v[:, part] = jnp.dot(
                    hid_v[...], weight_v[i], preferred_element_type=jnp.float32
                )
            else:
                out_v[:, part] = across(hid_v[...], weight_v[i])
            out_copies[i].start()
        for copy in out_copies:
            copy.wait()

    return pl.pallas_call(
        body,
        in_specs=[ANY] * (2 + len(after)),
        out_specs=ANY,
        out_shape=hbm_out((rows, width), jnp.float32),
        scratch_shapes=[
            pltpu.VMEM((rows, hidden), jnp.bfloat16),
            pltpu.VMEM((parts, hidden, cols) if stream == 0 else (parts, cols, hidden), jnp.bfloat16),
            pltpu.VMEM((rows, width), jnp.float32),
            pltpu.SemaphoreType.DMA(()),
            pltpu.SemaphoreType.DMA((parts,)),
            pltpu.SemaphoreType.DMA((parts,)),
        ],
        compiler_params=params(VMEM_MIB),
        cost_estimate=SMALL,
        name="share_of",
    )(hid, weight, *after)


def on_device(line, cols, tokens, w_in, w_out, out_grad):
    block, width = tokens.shape
    hidden = w_in.shape[1] // 2
    rows = min(ROWS, block)
    per = block // rows
    replica = lax.axis_index("dp").astype(jnp.int32).reshape(1)

    def ring_pairs(ring):
        up, down = ring * line, (1 - ring) * line
        pairs = [(up + i, up + i + 1) for i in range(line - 1)]
        pairs += [(down + i + 1, down + i) for i in range(line - 1)]
        return [*pairs, (up + line - 1, down + line - 1), (down, up)]

    def over_dp(x):
        return lax.ppermute(x, "dp", [(0, 1), (1, 0)])

    def over_col(x, k):
        return lax.ppermute(x, "col", [(i, i ^ k) for i in range(cols)])

    order = [(0, 0)] + [(d, k) for k in range(1, cols) for d in range(2)] + [(1, 0)]
    final = len(order) - 1
    count = len(order) * per
    ends = [count - count // 4, count]
    starts = [0, *ends[:-1]]

    last = []
    xg = {}
    partial = {}
    came = [[], []]
    kept = [()] * len(ends)
    shares = {}
    sums = [None, None]
    collected = {}

    def project_blocks(streams, parts):
        nonlocal last
        blocks = [part[1:] for part in parts]
        done = project(streams, blocks, (w_in, w_out), replica, hidden, last)
        for s, arrays in zip(streams, done, strict=True):
            for (b, _, _, n), array in zip(parts, arrays, strict=True):
                for i in range(n // rows):
                    partial.setdefault(b + i, [None, None, i * rows])[s] = array
        last = [done[-1][-1]]

    def project_one(r):
        project_blocks((0, 1), [(r * per, xg[order[r]], 0, block)])

    def step(ring, t):
        nonlocal last
        if t == 0:
            send = pack(partial[0][:2], last)
        else:
            terms = [partial[min(max(t - j, 0), count - 1)] for j in range(line)]
            send = chain_step(ring, came[ring][t - 1], terms, last)
        last = [send]
        came[ring].append(lax.ppermute(send, ("dp", "row"), ring_pairs(ring)))

    def gather_own():
        nonlocal last
        xg[0, 0] = pack((tokens, out_grad), last)
        last = [xg[0, 0]]
        for k in range(1, cols):
            if k & -k == k:
                xg[0, k] = over_col(xg[0, 0], k)
        xg[1, 0] = over_dp(xg[0, 0])

    def spread(k):
        nonlocal last
        xg[0, k] = hold(xg[0, k], last)
        last = [xg[0, k]]
        xg[1, k] = over_dp(xg[0, k])
        low = k & -k
        for j in range(1, low):
            if j & -j == j:
                xg[0, k | j] = over_col(xg[0, k], j)

    def activate_block(b):
        nonlocal last
        g = next(i for i, end in enumerate(ends) if b < end)
        got = [[came[ring][b + j] for j in range(line - 1)] for ring in range(2)]
        kept[g] = activate(
            partial[b],
            got,
            kept[g],
            (ends[g] - starts[g]) * rows,
            (b - starts[g]) * rows,
            last,
        )
        last = [kept[g][0]]

    def share_block(stream, r):
        nonlocal last
        b = r * per
        g = next(i for i, end in enumerate(ends) if b < end)
        shares[stream, r] = share_of(
            stream, kept[g][stream], (b - starts[g]) * rows, block, (w_out, w_in)[stream], last
        )
        last = [shares[stream, r]]

    def add_group(g, which):
        nonlocal last
        parts, b = [], starts[g]
        while b < ends[g]:
            until = min(ends[g], (b // per + 1) * per)
            part = xg[order[b // per]][which]
            parts.append(part[(b % per) * rows : (b % per + until - b) * rows])
            b = until
        outer = jnp.concatenate(parts) if len(parts) > 1 else parts[0]
        hid = kept[g][1 - which]
        sides = (outer, hid) if which == 0 else (hid, outer)
        term = lax.dot_general(*sides, (((0,), (0,)), ((), ())), preferred_element_type=jnp.float32)
        sums[which] = term if sums[which] is None else sums[which] + term
        last = [*last, sums[which]]

    def pair_sum(stream, k):
        nonlocal last
        both = shares[stream, 2 * k - 1] + over_dp(shares[stream, 2 * k])
        both = both.astype(jnp.bfloat16)
        last = [*last, both]
        collected[stream, k] = over_col(both, k)

    todo = {}

    def at(t, window, *what):
        todo.setdefault((t, window), []).append(what)

    own = (tokens, out_grad)
    at(0, 0, gather_own)
    if per > 1:
        at(0, 1, project_blocks, (0, 1), [(i, own, i * rows, rows) for i in range(1, per)])
    at(1, 0, project_one, final)
    for r in range(1, final):
        d, k = order[r]
        if cols <= 4:
            when, spread_when = r + 2, max(2 * k, 2)
        else:
            when, spread_when = 2 * r - 1, 2 * r - 2
        if d == 0 and k < 3:
            at(*divmod(spread_when, 2), spread, k)
        at(*divmod(when, 2), project_one, r)
        if d == 0 and k >= 3:
            at(*divmod(spread_when, 2), spread, k)
    for b in range(count):
        if b < count - 2:
            at(b + line, 0, activate_block, b)
        elif b == count - 2:
            at(b + line - 1, 1, activate_block, b)
    for r in range(final):
        t = (r + 1) * per - 1 + line
        early = t + 1 < count + line - 2
        for stream in range(2):
            when = t + stream if early else t
            at(when, 1, share_block, stream, r)
            if order[r][0] == 1:
                k = order[r][1]
                at(when + 1 if early else t, 1, pair_sum, stream, k)
                at(when + 2, 1, lambda stream=stream, k=k: last.append(collected[stream, k]))
    at(ends[0] + line, 0, add_group, 0, 0)
    at(ends[0] + line + 1, 0, add_group, 0, 1)

    def run(t, window):
        for what, *rest in todo.pop((t, window), []):
            what(*rest)

    project_blocks((0, 1), [(0, (tokens, out_grad), 0, rows)])
    for t in range(count + line - 2):
        for ring in range(2):
            step(ring, t)
            run(t, ring)
    for t, window in sorted(todo):
        run(t, window)
    activate_block(count - 1)
    results = []
    for stream in range(2):
        share_block(stream, final)
    add_group(len(ends) - 1, 0)
    add_group(len(ends) - 1, 1)

    for stream in range(2):
        total = shares[stream, 0]
        for k in range(1, cols):
            total = total + collected[stream, k].astype(jnp.float32)
        results.append((total + over_dp(shares[stream, final])).astype(jnp.bfloat16))
    grad_w_in, grad_w_out = (s.astype(jnp.bfloat16) for s in sums)
    return (*results, grad_w_in[:, None, :], grad_w_out[None])


def solution(mesh):
    placed = (P(("dp", "col"), "row"), P("row", "col"), P("col", "row"), P(("dp", "col"), "row"))
    return jax.shard_map(
        functools.partial(on_device, mesh.shape["row"], mesh.shape["col"]),
        mesh=mesh,
        in_specs=placed,
        out_specs=(
            P(("dp", "col"), "row"),
            P(("dp", "col"), "row"),
            P("row", "col", "dp"),
            P("col", "dp", "row"),
        ),
        check_vma=False,
    )
```

```python
import functools
import math

import jax
import jax.numpy as jnp
from jax import lax
from jax.experimental import pallas as pl
from jax.experimental.pallas import tpu as pltpu
from jax.sharding import PartitionSpec as P

ROWS = 128
VMEM_MIB = 64
REST_AT = (2, 0)
PROJECT_AT = ((1, 1), (2, 1), (4, 0), (5, 0), (7, 0), (9, 0), (11, 0))
PROJECT_COLS = 1024
PARTIAL = jnp.float32
ANY = pl.BlockSpec(memory_space=pltpu.HBM)
SMALL = pl.CostEstimate(flops=1024, bytes_accessed=1024, transcendentals=0)


def params(mib):
    return pltpu.CompilerParams(vmem_limit_bytes=mib << 20)


def hbm_out(shape, dtype=jnp.bfloat16):
    return jax.ShapeDtypeStruct(shape, dtype)


def row_chunks(rows, hidden):
    parts = 2 if rows % 32 == 0 and rows * hidden >= 1 << 17 else 1
    return [(i * (rows // parts), rows // parts) for i in range(parts)]


def across(left, right):
    return lax.dot_general(left, right, (((1,), (1,)), ((), ())), preferred_element_type=jnp.float32)


def project(streams, blocks, weights, replica, hidden, as_sent, after):
    width = blocks[0][0][0].shape[1]
    tile = min(PROJECT_COLS, hidden)
    steps = hidden // tile
    operands, specs, out_specs, out_shape = [], [], [], []
    types = [PARTIAL, jnp.bfloat16] if as_sent else [PARTIAL]
    for s in streams:
        operands.append(weights[s])
        if s == 0:
            specs.append(pl.BlockSpec((width, tile), lambda i, d: (0, d[0] * steps + i)))
        else:
            specs.append(pl.BlockSpec((tile, width), lambda i, d: (d[0] * steps + i, 0)))
        for pair, first, rows in blocks:
            at = first // rows
            if isinstance(pair, tuple):
                operands.append(pair[s])
                specs.append(pl.BlockSpec((rows, width), lambda i, d, at=at: (at, 0)))
            else:
                operands.append(pair)
                specs.append(pl.BlockSpec((None, rows, width), lambda i, d, s=s, at=at: (s, at, 0)))
            for out_type in types:
                out_specs.append(pl.BlockSpec((rows, tile), lambda i, d: (0, i)))
                out_shape.append(hbm_out((rows, hidden), out_type))

    def body(replica_ref, *refs):
        outs = iter(refs[len(operands) + len(after) :])
        given = iter(refs)
        for s in streams:
            weight = next(given)[...]
            for _ in blocks:
                x = next(given)[...]
                if s == 0:
                    value = jnp.dot(x, weight, preferred_element_type=jnp.float32)
                else:
                    value = across(x, weight)
                for _ in types:
                    out = next(outs)
                    out[...] = value.astype(out.dtype)

    return pl.pallas_call(
        body,
        grid_spec=pltpu.PrefetchScalarGridSpec(
            num_scalar_prefetch=1,
            grid=(steps,),
            in_specs=specs + [ANY] * len(after),
            out_specs=out_specs,
        ),
        out_shape=out_shape,
        compiler_params=params(VMEM_MIB),
        cost_estimate=SMALL,
        name="project",
    )(replica, *operands, *after)


def pack(pair, after):
    def body(*refs):
        out, held, in_sem, out_sem = refs[-4:]
        into = [pltpu.make_async_copy(refs[i], held.at[i], in_sem.at[i]) for i in range(2)]
        out_of = [pltpu.make_async_copy(held.at[i], out.at[i], out_sem.at[i]) for i in range(2)]
        for copy in into:
            copy.start()
        for i in range(2):
            into[i].wait()
            out_of[i].start()
        for copy in out_of:
            copy.wait()

    shape = (2, *pair[0].shape)
    return pl.pallas_call(
        body,
        in_specs=[ANY] * (2 + len(after)),
        out_specs=ANY,
        out_shape=hbm_out(shape),
        scratch_shapes=[
            pltpu.VMEM(shape, pair[0].dtype),
            pltpu.SemaphoreType.DMA((2,)),
            pltpu.SemaphoreType.DMA((2,)),
        ],
        compiler_params=params(VMEM_MIB),
        cost_estimate=SMALL,
        name="pack",
    )(*pair, *after)


def total_of(terms, after):
    rows, cols = terms[0][0].shape
    n = len(terms[0])

    def body(*refs):
        outs = refs[2 * n + len(after) :]
        for s in range(2):
            value = refs[s * n][...].astype(jnp.float32)
            for i in range(1, n):
                value = value + refs[s * n + i][...].astype(jnp.float32)
            outs[s][...] = value.astype(jnp.bfloat16)

    steps = 4 if rows % 64 == 0 else 1
    spec = pl.BlockSpec((rows // steps, cols), lambda i: (i, 0))
    return pl.pallas_call(
        body,
        grid=(steps,),
        in_specs=[spec] * (2 * n) + [ANY] * len(after),
        out_specs=[spec] * 2,
        out_shape=[hbm_out((rows, cols))] * 2,
        compiler_params=params(VMEM_MIB),
        cost_estimate=SMALL,
        name="total_of",
    )(*terms[0], *terms[1], *after)


def hold(array, after):
    return pl.pallas_call(
        lambda *refs: None,
        in_specs=[ANY] * (1 + len(after)),
        out_specs=ANY,
        out_shape=hbm_out(array.shape, array.dtype),
        input_output_aliases={0: 0},
        compiler_params=params(VMEM_MIB),
        cost_estimate=SMALL,
        name="hold",
    )(array, *after)


def own_place(ring, line):
    row = lax.axis_index("row")
    return jnp.where(lax.axis_index("dp") == ring, row, line - 1 - row)


def apart(after, arrays):
    return [a for a in after if all(a is not b for b in arrays)]


def distinct(arrays):
    found = []
    for array in arrays:
        if all(array is not seen for seen in found):
            found.append(array)
    return found, [next(i for i, seen in enumerate(found) if seen is a) for a in arrays]


def chain_step(got, partials, after):
    rows, hidden = got[0].shape
    late = len(partials)
    chunks = row_chunks(rows, hidden)
    arrays, which = distinct([array for array, _ in partials])

    def body(*refs):
        got_h, terms = refs[:2], refs[2 : 2 + len(arrays)]
        out_h = refs[2 + len(arrays) + len(after) :][:2]
        got_v, own_v, out_v, got_sem, own_sem, out_sem = refs[-6:]
        places = [own_place(ring, late) for ring in range(2)]

        def own_copy(j, ring, c):
            first, count = chunks[c]
            return pltpu.make_async_copy(
                terms[which[j]].at[pl.ds(partials[j][1] + first, count)],
                own_v.at[ring, pl.ds(first, count)],
                own_sem.at[ring, c],
            )

        for ring in range(2):
            for j in range(late):

                @pl.when(places[ring] == j)
                def _(ring=ring, j=j):
                    for c in range(len(chunks)):
                        own_copy(j, ring, c).start()

        copies = []
        for c, (first, count) in enumerate(chunks):
            part = pl.ds(first, count)
            for ring in range(2):
                got_copy = pltpu.make_async_copy(
                    got_h[ring].at[part], got_v.at[ring, part], got_sem.at[ring, c]
                )
                out_copy = pltpu.make_async_copy(
                    out_v.at[ring, part], out_h[ring].at[part], out_sem.at[ring, c]
                )
                got_copy.start()
                copies.append((ring, part, got_copy, own_copy(0, ring, c), out_copy))
        for ring, part, got_copy, mine, out_copy in copies:
            got_copy.wait()
            mine.wait()
            before = jnp.where(places[ring] == 0, 0.0, got_v[ring, part].astype(jnp.float32))
            out_v[ring, part] = (before + own_v[ring, part]).astype(out_v.dtype)
            out_copy.start()
        for copy in copies:
            copy[-1].wait()

    return pl.pallas_call(
        body,
        in_specs=[ANY] * (2 + len(arrays) + len(after)),
        out_specs=[ANY] * 2,
        out_shape=[hbm_out((rows, hidden))] * 2,
        scratch_shapes=[
            pltpu.VMEM((2, rows, hidden), jnp.bfloat16),
            pltpu.VMEM((2, rows, hidden), PARTIAL),
            pltpu.VMEM((2, rows, hidden), jnp.bfloat16),
        ]
        + [pltpu.SemaphoreType.DMA((2, len(chunks)))] * 3,
        compiler_params=params(VMEM_MIB),
        cost_estimate=SMALL,
        name="chain_step",
    )(*got, *arrays, *after)


def activate(partial, got, kept, kept_rows, kept_row, after):
    rows, hidden = got[0][0][0].shape
    line = len(got[0][0]) + 1
    after = apart(after, kept)
    given, which = distinct([*partial[:2], *(a for ring in got for stream in ring for a in stream)])
    step_rows, step_cols = 16, min(512, hidden)
    halves = len(row_chunks(rows, hidden))
    part_rows = rows // halves
    across_cols = hidden // step_cols
    tiles = (part_rows // step_rows) * across_cols

    def body(*refs):
        terms = refs[: len(given)]
        outs = refs[len(given) + len(kept) + len(after) :][:2]
        own_v, got_v, out_v, own_sem, got_sem, out_sem = refs[-6:]

        def own_copy(s, h):
            part = pl.ds(h * part_rows, part_rows)
            return pltpu.make_async_copy(
                terms[which[s]].at[pl.ds(partial[2] + h * part_rows, part_rows)],
                own_v.at[s, part],
                own_sem.at[s, h],
            )

        def got_copy(ring, j, s, h):
            part = pl.ds(h * part_rows, part_rows)
            return pltpu.make_async_copy(
                terms[which[2 + (2 * ring + s) * (line - 1) + j]].at[part],
                got_v.at[ring, s, part],
                got_sem.at[ring, s, h],
            )

        for h in range(halves):
            for s in range(2):
                own_copy(s, h).start()
                for ring in range(2):
                    place = own_place(ring, line)

                    @pl.when(place == 0)
                    def _(ring=ring, s=s, h=h):
                        part = pl.ds(h * part_rows, part_rows)
                        got_v[ring, s, part] = jnp.zeros((part_rows, hidden), got_v.dtype)

                    for j in range(1, line):

                        @pl.when(place == j)
                        def _(ring=ring, j=j, s=s, h=h):
                            got_copy(ring, j - 1, s, h).start()

        out_copies = []
        for h in range(halves):
            for s in range(2):
                own_copy(s, h).wait()
                for ring in range(2):

                    @pl.when(own_place(ring, line) != 0)
                    def _(ring=ring, s=s, h=h):
                        got_copy(ring, 0, s, h).wait()

            def tile(i, _, h=h):
                at = pl.multiple_of((i // across_cols) * step_rows, step_rows)
                r = pl.ds(h * part_rows + at, step_rows)
                c = pl.ds(pl.multiple_of((i % across_cols) * step_cols, step_cols), step_cols)
                pre, grad = (
                    own_v[s, r, c].astype(jnp.float32)
                    + got_v[0, s, r, c].astype(jnp.float32)
                    + got_v[1, s, r, c].astype(jnp.float32)
                    for s in range(2)
                )
                cdf = 0.5 * (1.0 + lax.erf(pre * (1.0 / math.sqrt(2.0))))
                pdf = jnp.exp(-0.5 * pre * pre) * (1.0 / math.sqrt(2.0 * math.pi))
                out_v[0, r, c] = (pre * cdf).astype(jnp.bfloat16)
                out_v[1, r, c] = (grad * (cdf + pre * pdf)).astype(jnp.bfloat16)
                return 0

            lax.fori_loop(0, tiles, tile, 0)
            for i in range(2):
                copy = pltpu.make_async_copy(
                    out_v.at[i, pl.ds(h * part_rows, part_rows)],
                    outs[i].at[pl.ds(kept_row + h * part_rows, part_rows)],
                    out_sem.at[i, h],
                )
                copy.start()
                out_copies.append(copy)
        for copy in out_copies:
            copy.wait()

    return pl.pallas_call(
        body,
        in_specs=[ANY] * (len(given) + len(kept) + len(after)),
        out_specs=[ANY] * 2,
        out_shape=[hbm_out((kept_rows, hidden))] * 2,
        input_output_aliases={len(given) + i: i for i in range(len(kept))},
        scratch_shapes=[
            pltpu.VMEM((2, rows, hidden), PARTIAL),
            pltpu.VMEM((2, 2, rows, hidden), jnp.bfloat16),
            pltpu.VMEM((2, rows, hidden), jnp.bfloat16),
            pltpu.SemaphoreType.DMA((2, halves)),
            pltpu.SemaphoreType.DMA((2, 2, halves)),
            pltpu.SemaphoreType.DMA((2, halves)),
        ],
        compiler_params=params(VMEM_MIB),
        cost_estimate=SMALL,
        name="activate",
    )(*given, *kept, *after)


def share_of(hid, first, rows, weights, out_type, after):
    hidden = hid[0].shape[1]
    width = weights[0].shape[1]

    def body(*refs):
        hid_h, weight_h = refs[:2], refs[2:4]
        out_h = refs[4 + len(after) :][:2]
        hid_v, w_out_v, w_in_v, out_v, hid_sem, weight_sem, out_sem = refs[-7:]
        mine = pl.ds(pl.multiple_of(lax.axis_index("dp") * hidden, hidden), hidden)
        part = pl.ds(first, rows)
        hid_copies = [
            pltpu.make_async_copy(hid_h[i].at[part], hid_v.at[i], hid_sem.at[i]) for i in range(2)
        ]
        weight_copies = [
            pltpu.make_async_copy(weight_h[0].at[mine], w_out_v, weight_sem.at[0]),
            pltpu.make_async_copy(weight_h[1].at[:, mine], w_in_v, weight_sem.at[1]),
        ]
        out_copies = [
            pltpu.make_async_copy(out_v.at[i], out_h[i], out_sem.at[i]) for i in range(2)
        ]
        for i in range(2):
            hid_copies[i].start()
            weight_copies[i].start()
        for i in range(2):
            hid_copies[i].wait()
            weight_copies[i].wait()
            if i == 0:
                value = jnp.dot(hid_v[0], w_out_v[...], preferred_element_type=jnp.float32)
            else:
                value = across(hid_v[1], w_in_v[...])
            out_v[i] = value.astype(out_type)
            out_copies[i].start()
        for copy in out_copies:
            copy.wait()

    return pl.pallas_call(
        body,
        in_specs=[ANY] * (4 + len(after)),
        out_specs=[ANY] * 2,
        out_shape=[hbm_out((rows, width), out_type)] * 2,
        scratch_shapes=[
            pltpu.VMEM((2, rows, hidden), jnp.bfloat16),
            pltpu.VMEM((hidden, width), jnp.bfloat16),
            pltpu.VMEM((width, hidden), jnp.bfloat16),
            pltpu.VMEM((2, rows, width), out_type),
            pltpu.SemaphoreType.DMA((2,)),
            pltpu.SemaphoreType.DMA((2,)),
            pltpu.SemaphoreType.DMA((2,)),
        ],
        compiler_params=params(VMEM_MIB),
        cost_estimate=SMALL,
        name="share_of",
    )(*hid, *weights, *after)


def add_pair(left, right, after):
    rows, cols = left.shape

    def body(left_ref, right_ref, *rest):
        rest[-1][...] = (left_ref[...] + right_ref[...].astype(jnp.float32)).astype(jnp.bfloat16)

    steps = 2 if rows % 32 == 0 else 1
    spec = pl.BlockSpec((rows // steps, cols), lambda i: (i, 0))
    return pl.pallas_call(
        body,
        grid=(steps,),
        in_specs=[spec, spec] + [ANY] * len(after),
        out_specs=spec,
        out_shape=hbm_out((rows, cols)),
        compiler_params=params(VMEM_MIB),
        cost_estimate=SMALL,
        name="add_pair",
    )(left, right, *after)


def gradients(blocks, hid, after):
    _, block, width = blocks[0].shape
    depth, hidden = hid[0].shape
    n = len(blocks)
    given = [*blocks, *hid]
    sizes = [(width, hidden), (hidden, width)]
    tall = min(512, width, hidden)

    def body(*refs):
        act_h, grad_h = refs[n : n + 2]
        out_h = refs[len(given) + len(after) :][:2]
        x_v, grad_v, act_v, g_v, in_v, out_v, block_sem, hid_sem, in_sem, out_sem = refs[-10:]
        sides = [(x_v, grad_h, grad_v), (g_v, act_h, act_v)]
        copies = [[], []]
        for which, (blocks_v, hid_h, hid_v) in enumerate(sides):
            for i in range(n):
                rows = pl.ds(i * block, block)
                copies[which] += [
                    pltpu.make_async_copy(
                        refs[i].at[which], blocks_v.at[rows], block_sem.at[which, i]
                    ),
                    pltpu.make_async_copy(hid_h.at[rows], hid_v.at[rows], hid_sem.at[which, i]),
                ]
            for copy in copies[which]:
                copy.start()
        done = []
        for which, (left, right, result_v, sem) in enumerate(
            [(x_v, grad_v, in_v, in_sem), (act_v, g_v, out_v, out_sem)]
        ):
            for copy in copies[which]:
                copy.wait()

            def part(i, _, left=left, right=right, result_v=result_v, sem=sem, which=which):
                rows = pl.ds(pl.multiple_of(i * tall, tall), tall)
                result_v[rows] = lax.dot_general(
                    left[:, rows],
                    right[...],
                    (((0,), (0,)), ((), ())),
                    preferred_element_type=jnp.float32,
                ).astype(jnp.bfloat16)
                pltpu.make_async_copy(result_v.at[rows], out_h[which].at[rows], sem.at[i]).start()
                return 0

            lax.fori_loop(0, sizes[which][0] // tall, part, 0)
            for i in range(sizes[which][0] // tall):
                rows = pl.ds(i * tall, tall)
                done.append(
                    pltpu.make_async_copy(result_v.at[rows], out_h[which].at[rows], sem.at[i])
                )
        for copy in done:
            copy.wait()

    return pl.pallas_call(
        body,
        in_specs=[ANY] * (len(given) + len(after)),
        out_specs=[ANY] * 2,
        out_shape=[hbm_out(size) for size in sizes],
        scratch_shapes=[
            pltpu.VMEM((depth, width), jnp.bfloat16),
            pltpu.VMEM((depth, hidden), jnp.bfloat16),
            pltpu.VMEM((depth, hidden), jnp.bfloat16),
            pltpu.VMEM((depth, width), jnp.bfloat16),
            pltpu.VMEM(sizes[0], jnp.bfloat16),
            pltpu.VMEM(sizes[1], jnp.bfloat16),
            pltpu.SemaphoreType.DMA((2, n)),
            pltpu.SemaphoreType.DMA((2, n)),
            pltpu.SemaphoreType.DMA((width // tall,)),
            pltpu.SemaphoreType.DMA((hidden // tall,)),
        ],
        compiler_params=params(VMEM_MIB),
        cost_estimate=SMALL,
        name="gradients",
    )(*given, *after)


def on_device(line, cols, tokens, w_in, w_out, out_grad):
    block, width = tokens.shape
    hidden = w_in.shape[1] // 2
    rows = min(ROWS, block)
    per = block // rows
    replica = lax.axis_index("dp").astype(jnp.int32).reshape(1)

    def ring_pairs(ring):
        up, down = ring * line, (1 - ring) * line
        pairs = [(up + i, up + i + 1) for i in range(line - 1)]
        pairs += [(down + i + 1, down + i) for i in range(line - 1)]
        return [*pairs, (up + line - 1, down + line - 1), (down, up)]

    def over_dp(x):
        return lax.ppermute(x, "dp", [(0, 1), (1, 0)])

    def over_col(x, k):
        return lax.ppermute(x, "col", [(i, i ^ k) for i in range(cols)])

    order = [(0, 0)] + [(d, k) for k in range(1, cols) for d in range(2)] + [(1, 0)]
    final = len(order) - 1
    count = len(order) * per
    last = []
    own = (tokens, out_grad)
    xg = {(0, 0): own}
    first = {}
    partial = {}
    came = [[[], []], [[], []]]
    kept = ()
    shares = {}
    swapped = {}
    pairs = {}
    collected = {}

    def project_blocks(streams, parts, as_sent=False):
        nonlocal last
        blocks = [part[1:] for part in parts]
        done = project(streams, blocks, (w_in, w_out), replica, hidden, as_sent, last)
        arrays = iter(done)
        for s in streams:
            for b, _, _, n in parts:
                array = next(arrays)
                for i in range(n // rows):
                    partial.setdefault(b + i, [None, None, i * rows])[s] = array
                if as_sent:
                    first[s] = next(arrays)
        last = [done[-1]]

    def project_one(r):
        project_blocks((0, 1), [(r * per, xg[order[r]], 0, block)])

    def step(stream, t):
        nonlocal last
        if t == 0:
            send = [first[stream]] * 2
        else:
            terms = [partial[min(max(t - j, 0), count - 1)] for j in range(line)]
            got = [came[ring][stream][t - 1] for ring in range(2)]
            send = chain_step(got, [(term[stream], term[2]) for term in terms], last)
        last = [send[0]]
        for ring in range(2):
            came[ring][stream].append(lax.ppermute(send[ring], ("dp", "row"), ring_pairs(ring)))

    def gather_own():
        nonlocal last
        xg[0, 0] = pack(own, last)
        last = [xg[0, 0]]
        spread_from(1, cols if not staged else 2)

    def spread_from(first_k, end):
        for k in range(first_k, end):
            low = k & -k
            xg[0, k] = over_col(xg[0, k ^ low], low)
        for k in range(first_k, end):
            xg[1, k] = over_dp(xg[0, k])
        if end == cols:
            xg[1, 0] = over_dp(xg[0, 0])

    def gather_rest():
        nonlocal last
        xg[0, 0] = hold(xg[0, 0], last)
        last = [xg[0, 0]]
        spread_from(2, cols)

    def activate_block(b):
        nonlocal last, kept
        got = [
            [[came[ring][s][b + j] for j in range(line - 1)] for s in range(2)] for ring in range(2)
        ]
        kept = activate(partial[b], got, kept, count * rows, b * rows, last)
        last = [kept[0]]

    def share_block(r):
        nonlocal last
        d, k = order[r]
        out_type = jnp.float32 if d == 0 else jnp.bfloat16
        shares[r] = share_of(kept, r * block, block, (w_out, w_in), out_type, last)
        last = [shares[r][0]]

    def swap(stream, k, later):
        nonlocal last
        array = shares[order.index((1, k))][stream]
        if later:
            array = hold(array, last)
            last = [array]
        swapped[stream, k] = over_dp(array)

    def pair_sum(stream, k):
        nonlocal last
        pairs[stream, k] = add_pair(shares[2 * k - 1][stream], swapped[stream, k], last)
        last = [pairs[stream, k]]

    def send_pair(stream, k, later):
        nonlocal last
        array = pairs[stream, k]
        if later:
            array = hold(array, last)
            last = [array]
        collected[stream, k] = over_col(array, k)

    def come_after(stream, k):
        last.append(collected[stream, k])

    todo = {}

    def at(t, window, *what):
        todo.setdefault((t, window), []).append(what)

    at(0, 0, gather_own)
    if per > 1:
        at(0, 1, project_blocks, (0, 1), [(i, own, i * rows, rows) for i in range(1, per)])
    staged = cols == 4 and per == 2
    if staged:
        at(REST_AT[0], REST_AT[1], gather_rest)
        for r, when in enumerate(PROJECT_AT):
            at(*when, project_one, r + 1)
    else:
        for r in range(1, len(order)):
            at(r * per - 1, 0, project_one, r)
    for b in range(count - 1):
        at(b + line - 1, 1, activate_block, b)
    for r in range(final):
        d, k = order[r]
        t = (r + 1) * per + line - 2
        at(t, 1, share_block, r)
        if d == 1 and r < final - 1:
            at(t, 1, swap, 0, k, False)
            at(t + 1, 1, pair_sum, 0, k)
            at(t + 1, 1, swap, 1, k, True)
            at(t + 2, 1, pair_sum, 1, k)
            at(t + 2, 1, send_pair, 0, k, True)
            at(t + 3, 1, come_after, 0, k)
            at(t + 3, 1, send_pair, 1, k, True)
            at(t + 4, 1, come_after, 1, k)
        elif d == 1:
            for stream in range(2):
                at(t, 1, swap, stream, k, False)
                at(t + 1, 1, pair_sum, stream, k)
                at(t + 1, 1, send_pair, stream, k, False)

    def run(t, window):
        for what, *rest in todo.pop((t, window), []):
            what(*rest)

    for t in range(count + line - 2):
        for stream in range(2):
            if t == 0:
                project_blocks((stream,), [(0, own, 0, rows)], True)
            step(stream, t)
            run(t, stream)
    for t, window in sorted(todo):
        run(t, window)
    activate_block(count - 1)
    share_block(final)
    for stream in range(2):
        swap(stream, 0, False)
    grad_w_in, grad_w_out = gradients([xg[d_k] for d_k in order], kept, last)

    terms = [
        [shares[0][s], *(collected[s, k] for k in range(1, cols)), swapped[s, 0]] for s in range(2)
    ]
    output, grad_x = total_of(terms, [grad_w_in])
    return (output, grad_x, grad_w_in[:, None, :], grad_w_out[None])


def solution(mesh):
    placed = (P(("dp", "col"), "row"), P("row", "col"), P("col", "row"), P(("dp", "col"), "row"))
    return jax.shard_map(
        functools.partial(on_device, mesh.shape["row"], mesh.shape["col"]),
        mesh=mesh,
        in_specs=placed,
        out_specs=(
            P(("dp", "col"), "row"),
            P(("dp", "col"), "row"),
            P("row", "col", "dp"),
            P("col", "dp", "row"),
        ),
        check_vma=False,
    )
```
